256 devices in a mesh: walk: 64 (over x, z, core), vec: 4 (over y).
Axes of the slice: x: 4, y: 4, z: 8, core: 2. Of those that a mesh axis runs over, the one named last changes fastest.
Arguments:
- walkers: bfloat16 [128, 2432, 768], P('walk')
- chol: bfloat16 [4, 64, 384, 4096], P('vec', 'walk'), may hold values from -6 to 6
- owners: int32 [4, 2], P('vec'), may hold values from 0 to 63
- branch_src: int32 [128], P('walk'), may hold values from 0 to 127, as said below
Outputs:
- branched: bfloat16 [128, 2432, 768], P('walk')
- force_bias: float32 [128, 8, 2], P('walk', 'vec')
- exchange: float32 [128, 2], P('walk')
The draws below stay inside these ranges and needn't reach their ends.
Inputs may be any that keep to these rules, and one draw needn't show every extreme that they name: `branch_src`: slot s takes its walker from the 2 walkers of block s // 2, or of the block before or after it (blocks taken cyclically).
All inputs are finite; a program needn't handle non-finite values.
Results may differ from the reference program's by a relative error of at most 0.0052.
Values may be sent and summed in bfloat16 or wider, within the bound.
No kernel may reach another device: no remote copies, remote signals or barrier semaphores. Data moves between devices by JAX's collectives and lax.ppermute only.
A program may use at most 192 MiB of HBM per device.

```python
import jax
import jax.numpy as jnp
from jax import lax

NORB = 2048
NE = 384
W_DEV = 2
G_USE = 2
WALKERS = 128
N_WALK = 64
N_VEC = 4


def draw_walkers(key, part):
    first, second = jax.random.split(key)
    orbital = jax.random.normal(first, (WALKERS, NORB, 2 * NE), jnp.float32)
    inverse = jax.random.normal(second, (WALKERS, NE, 2 * NE), jnp.float32)
    orbital = orbital * NORB ** (-0.5)
    inverse = inverse * (0.5 / NE)
    return jnp.concatenate([orbital, inverse], axis=1).astype(jnp.bfloat16)


def draw_branch_src(key, part):
    first, second = jax.random.split(key)
    slots = jnp.arange(WALKERS, dtype=jnp.int32)
    blocks = slots // W_DEV
    offset = jax.random.randint(first, (WALKERS,), -1, 2, dtype=jnp.int32)
    within = jax.random.randint(second, (WALKERS,), 0, W_DEV, dtype=jnp.int32)
    count = WALKERS // W_DEV
    return ((blocks + offset + count) % count * W_DEV + within).astype(jnp.int32)


def set_ends(values, own_key, low, high):
    index_at = [jax.random.randint(jax.random.fold_in(own_key, axis), (), 0, length) for axis, length in enumerate(values.shape)]
    widest = values.shape.index(max(values.shape))
    beside = index_at[:widest] + [(index_at[widest] + 1) % values.shape[widest]] + index_at[widest + 1:]
    return values.at[tuple(index_at)].set(low).at[tuple(beside)].set(high)


def steps_of(rng, shape, cuts, least, high):
    gain, own = 1.0, jax.random.fold_in(rng, 6)
    for position, blocks in cuts:
        draws = jnp.exp(jax.random.uniform(jax.random.fold_in(own, position), (blocks,), jnp.float32, least / len(cuts), high / len(cuts)))
        gain = gain * jnp.repeat(draws, shape[position] // blocks).reshape([-1 if axis == position else 1 for axis in range(len(shape))])
    return gain


def normal_values(stream_key, dims, scale, bound, shards=(), held_as=jnp.bfloat16):
    entries = jax.random.normal(stream_key, dims, jnp.float32) * scale
    if len(shards) > 0:
        entries = steps_of(stream_key, dims, shards, -0.22, 0.18) * entries
    return jnp.clip(entries, min=-bound, max=bound).astype(held_as)


def setup_inputs(seed: int = 0) -> dict:
    arg_keys = jax.random.split(jax.random.key(seed), 5)
    return {
        "walkers": draw_walkers(jax.random.fold_in(arg_keys[4], 71), 0),
        "chol": normal_values(arg_keys[1], (N_VEC, N_WALK, NE, 2 * NORB), 1.0, 6.0, ((0, 4), (1, 64))),
        "owners": set_ends(jax.random.randint(arg_keys[2], (N_VEC, G_USE), 0, N_WALK), jax.random.fold_in(arg_keys[2], 1), 0, N_WALK - 1).astype(jnp.int32),
        "branch_src": draw_branch_src(jax.random.fold_in(arg_keys[4], 71), 0),
    }


def complex_block(part):
    half = part.shape[1] // 2
    lower = jnp.concatenate([-part[:, half:], part[:, :half]], axis=1)
    return jnp.concatenate([part, lower], axis=0)


def reference(walkers, chol, owners, branch_src):
    branched = walkers[branch_src]
    picked = chol[jnp.arange(N_VEC)[:, None], owners]
    stacked = picked.reshape(N_VEC * G_USE * NE, 2 * NORB)

    def per_walker(state):
        pbig = complex_block(state[:NORB])
        obig = complex_block(state[NORB:]).astype(jnp.float32)
        mixed = jnp.dot(stacked, pbig, preferred_element_type=jnp.float32).astype(jnp.bfloat16)
        mixed = mixed.reshape(N_VEC * G_USE, NE, 2 * NE).astype(jnp.float32)
        green = jnp.einsum('gik,kj->gij', mixed, obig, precision=lax.Precision.HIGHEST)
        real = green[:, :, :NE]
        imag = green[:, :, NE:]
        bias = jnp.stack([jnp.trace(real, axis1=1, axis2=2), jnp.trace(imag, axis1=1, axis2=2)], axis=1)
        real_t = jnp.swapaxes(real, 1, 2)
        imag_t = jnp.swapaxes(imag, 1, 2)
        ex_real = jnp.sum(real * real_t - imag * imag_t)
        ex_imag = 2.0 * jnp.sum(real * imag_t)
        return bias, -0.5 * jnp.stack([ex_real, ex_imag])

    force_bias, exchange = lax.map(per_walker, branched)
    return branched, force_bias, exchange
```

```python
import jax
import jax.numpy as jnp
from jax import lax
from jax.experimental import pallas as pl
from jax.experimental.pallas import tpu as pltpu
from jax.sharding import PartitionSpec as P

NX, NZ, NC, NY = 4, 8, 2, 4


def walk_index(x, z, c):
    return ((x % NX) * NZ + z % NZ) * NC + c % NC


def chips():
    return [(x, z, c) for x in range(NX) for z in range(NZ) for c in range(NC)]


def chip_shift(dx, dz, dc):
    return [(walk_index(x, z, c), walk_index(x + dx, z + dz, c + dc)) for x, z, c in chips()]


def ring(size, step):
    return [(i, (i + step) % size) for i in range(size)]


def across_chips():
    size = NX * NZ * NC
    return [(i, (i + 1) % size if i % NC == 1 else (i - 1) % size) for i in range(size)]


def terms_kernel(place_ref, *refs):
    pieces, (w_ref, out_ref, acc_ref, m_ref) = refs[:2 * NX], refs[2 * NX:]
    half, depth = pieces[0].shape
    electrons, orbitals = NC * half, 2 * depth
    for side in range(NC):
        acc_ref[...] = jnp.zeros_like(acc_ref)
        for k in range(NX):
            block = place_ref[k]
            rows = pl.ds(pl.multiple_of(lax.rem(block, 2) * depth, depth), depth)
            acc_ref[lax.div(block, 2)] += jnp.dot(
                pieces[side * NX + k][...], w_ref[0, rows, :], preferred_element_type=jnp.float32
            )
        by_real, by_imag = acc_ref[0], acc_ref[1]
        place = pl.ds(pl.multiple_of(place_ref[NX + side] * half, half), half)
        m_ref[0, place, :] = (by_real[:, :electrons] - by_imag[:, electrons:]).astype(jnp.bfloat16)
        m_ref[1, place, :] = (by_real[:, electrons:] + by_imag[:, :electrons]).astype(jnp.bfloat16)
    inverse = w_ref[0, orbitals:, :]
    g_by_real = jnp.dot(m_ref[0], inverse, preferred_element_type=jnp.float32)
    g_by_imag = jnp.dot(m_ref[1], inverse, preferred_element_type=jnp.float32)
    real = g_by_real[:, :electrons] - g_by_imag[:, electrons:]
    imag = g_by_real[:, electrons:] + g_by_imag[:, :electrons]
    real_t = real.T
    rows = lax.broadcasted_iota(jnp.int32, real.shape, 0)
    columns = lax.broadcasted_iota(jnp.int32, real.shape, 1)
    diagonal = rows == columns
    values = (
        jnp.sum(jnp.where(diagonal, real, 0.0)),
        jnp.sum(jnp.where(diagonal, imag, 0.0)),
        jnp.sum(real * real_t - imag * imag.T),
        2.0 * jnp.sum(imag * real_t),
    )
    lane = lax.broadcasted_iota(jnp.int32, out_ref.shape, 2)
    row = jnp.zeros(out_ref.shape, jnp.float32)
    for place, value in enumerate(values):
        row = jnp.where(lane == place, value, row)
    out_ref[...] = row


def walker_terms(place, pieces, walkers):
    count, height, width = walkers.shape
    half, depth = pieces[0].shape
    electrons = NC * half
    whole = pl.BlockSpec((half, depth), lambda i, _: (0, 0))
    out = pl.pallas_call(
        terms_kernel,
        grid_spec=pltpu.PrefetchScalarGridSpec(
            num_scalar_prefetch=1,
            grid=(count,),
            in_specs=[whole] * len(pieces) + [pl.BlockSpec((1, height, width), lambda i, _: (i, 0, 0))],
            out_specs=pl.BlockSpec((1, 8, 128), lambda i, _: (i, 0, 0)),
            scratch_shapes=[
                pltpu.VMEM((2, half, width), jnp.float32),
                pltpu.VMEM((2, electrons, width // 2), jnp.bfloat16),
            ],
        ),
        out_shape=jax.ShapeDtypeStruct((count, 8, 128), jnp.float32),
        compiler_params=pltpu.CompilerParams(vmem_limit_bytes=56 * 2**20),
        cost_estimate=pl.CostEstimate(
            flops=2 * count * electrons * (2 * NX * depth // 2 + width) * width,
            bytes_accessed=2 * (len(pieces) * pieces[0].size + walkers.size),
            transcendentals=0,
        ),
    )(place, *pieces, walkers)
    return out[:, 0, :4]


def branch_kernel(plan_ref, own_ref, core_ref, q0_ref, q1_ref, q2_ref, q3_ref, out_ref, held, in_sems, out_sems):
    slots, height, _ = out_ref.shape
    part = height // NY
    quarters = (q0_ref, q1_ref, q2_ref, q3_ref)

    def rows(k):
        return pl.ds(pl.multiple_of(plan_ref[2 * slots + k] * part, 16), part)

    def fetch(slot, k, source, index):
        src = (own_ref.at[index, rows(k)], core_ref.at[index, rows(k)], quarters[k].at[index])[source]
        return pltpu.make_async_copy(src, held.at[slot, k], in_sems.at[slot, k])

    def store(slot, k):
        return pltpu.make_async_copy(held.at[slot, k], out_ref.at[slot, rows(k)], out_sems.at[slot, k])

    for slot in range(slots):
        index = plan_ref[slots + slot]
        for source in range(3):
            @pl.when(plan_ref[slot] == source)
            def _(slot=slot, index=index, source=source):
                for k in range(NY):
                    fetch(slot, k, source, index).start()
    for slot in range(slots):
        for k in range(NY):
            fetch(slot, k, 0, 0).wait()
            store(slot, k).start()
    for slot in range(slots):
        for k in range(NY):
            store(slot, k).wait()


def branch(plan, own, other_core, quarters):
    anywhere = pl.BlockSpec(memory_space=pl.ANY)
    slots, height, width = own.shape
    return pl.pallas_call(
        branch_kernel,
        in_specs=[pl.BlockSpec(memory_space=pltpu.SMEM)] + [anywhere] * 6,
        out_specs=anywhere,
        out_shape=jax.ShapeDtypeStruct(own.shape, own.dtype),
        scratch_shapes=[
            pltpu.VMEM((slots, NY, height // NY, width), own.dtype),
            pltpu.SemaphoreType.DMA((slots, NY)),
            pltpu.SemaphoreType.DMA((slots, NY)),
        ],
        compiler_params=pltpu.CompilerParams(vmem_limit_bytes=56 * 2**20),
        cost_estimate=pl.CostEstimate(flops=0, bytes_accessed=4 * own.size, transcendentals=0),
    )(plan, own, other_core, *quarters)


def after(values, *done):
    return jax.tree.unflatten(
        jax.tree.structure(values), lax.optimization_barrier((*jax.tree.leaves(values), *done))[: len(jax.tree.leaves(values))]
    )


def cut_blocks(own, swapped, owner, x, c):
    electrons, columns = own.shape
    half, depth = electrons // NC, columns // NX

    def block(place):
        cut = [lax.dynamic_slice(a, (c * half, place * depth), (half, depth)) for a in (own, swapped)]
        return jnp.where(owner % NC == c, cut[0], cut[1])

    return [block((x + dx) % NX) for dx in (0, 1, 3, 2)]


def scattered(blocks, owner, x):
    piece = blocks[0]
    for dx, sent in zip((1, 3, 2), blocks[1:]):
        arrived = lax.ppermute(sent, "walk", chip_shift(dx, 0, 0))
        piece = jnp.where((owner // (NZ * NC) + dx) % NX == x, arrived, piece)
    return piece


def flood_step(step, halves, streams, is_owner):
    up, down = streams[-1] if streams else halves
    if step == 2:
        up, down = jnp.where(is_owner, halves[1], up), jnp.where(is_owner, halves[0], down)
    return lax.ppermute(up, "walk", chip_shift(0, 1, 0)), lax.ppermute(down, "walk", chip_shift(0, -1, 0))


def flooded(halves, streams, away):
    first, second = halves
    for step, (up, down) in enumerate(streams, 1):
        first = jnp.where(away == step, up, first)
        second = jnp.where(away == NZ - step, down, second)
        if step > 1:
            first = jnp.where(away == NZ - (step - 1), down, first)
            second = jnp.where(away == step - 1, up, second)
    return jnp.concatenate([first, second], axis=0)


def along_x(piece):
    return [lax.ppermute(piece, "walk", chip_shift(dx, 0, 0)) for dx in (1, 3, 2)]


def to_other_core(array):
    return lax.ppermute(array, "walk", chip_shift(0, 0, 1))


def shards(walkers, chol, owners, branch_src):
    slots, height, _ = walkers.shape
    device, y = lax.axis_index("walk"), lax.axis_index("vec")
    x, z, c = device // (NZ * NC), device // NC % NZ, device % NC
    size = NX * NZ * NC
    total = slots * size
    own = chol[0, 0]
    owner = owners[0]
    steps = range(1, NZ // 2 + 1)
    both_ways = [
        (w * NY + v, w * NY + (v + (1 if w % NC == 0 else -1)) % NY) for w in range(size) for v in range(NY)
    ]

    def pass_on(quarter):
        return lax.ppermute(quarter, ("walk", "vec"), both_ways)

    with jax.named_scope("core_swap"):
        swapped = to_other_core(own)
    with jax.named_scope("halo_z"):
        part = height // NY
        quarters = [lax.ppermute(lax.dynamic_slice_in_dim(walkers, y * part, part, 1), "walk", across_chips())]
    with jax.named_scope("blocks"):
        blocks = [cut_blocks(own, swapped, owner[g], x, c) for g in range(2)]
    half = own.shape[0] // (2 * NC)
    halves, streams = [None, None], [[], []]
    is_owner = [owner[g] // NC % NZ == z for g in range(2)]
    with jax.named_scope("x_scatter_0"):
        piece = scattered(blocks[0], owner[0], x)
        halves[0] = (piece[:half], piece[half:])
    with jax.named_scope("core_walkers"):
        other_core = to_other_core(after(walkers, piece))
    with jax.named_scope("x_scatter_1"):
        piece = scattered(after(blocks[1], *halves[0]), owner[1], x)
    with jax.named_scope("z_flood_0"):
        for step in (1, 2):
            streams[0].append(flood_step(step, halves[0], streams[0], is_owner[0]))
    with jax.named_scope("halo_y"):
        quarters.append(pass_on(after(quarters[0], *streams[0][0])))
    with jax.named_scope("z_flood_1"):
        halves[1] = after((piece[:half], piece[half:]), *streams[0][1])
        streams[1].append(flood_step(1, halves[1], streams[1], is_owner[1]))
    with jax.named_scope("z_flood_0"):
        for step in (3, 4):
            streams[0].append(flood_step(step, halves[0], streams[0], is_owner[0]))
        piece = flooded(halves[0], streams[0], (z - owner[0] // NC + NZ * NX) % NZ)
    with jax.named_scope("x_gather_0"):
        mine = [piece] + along_x(piece)
    with jax.named_scope("z_flood_1"):
        streams[1][0] = after(streams[1][0], quarters[1])
        for step in (2, 3, 4):
            streams[1].append(flood_step(step, halves[1], streams[1], is_owner[1]))
        piece = flooded(halves[1], streams[1], (z - owner[1] // NC + NZ * NX) % NZ)
    with jax.named_scope("halo_y"):
        quarters.append(pass_on(quarters[1]))
    with jax.named_scope("core_gather_0"):
        pieces = mine + [to_other_core(p) for p in mine]
    with jax.named_scope("x_gather_1"):
        piece = after(piece, quarters[2], *mine)
        mine = [piece] + along_x(piece)
    with jax.named_scope("halo_y"):
        quarters.append(pass_on(quarters[2]))
    relative = (branch_src - (device - 1) * slots + total) % total
    side, index = relative // slots, relative % slots
    source = jnp.where(side == 1, 0, jnp.where((side == 0) == (c == 0), 2, 1))
    held = (y + jnp.arange(NY) * jnp.where(c == 0, NY - 1, 1)) % NY
    plan = jnp.concatenate([source, index, held]).astype(jnp.int32)
    place = jnp.stack([x, (x + 3) % NX, (x + 1) % NX, (x + 2) % NX, c, 1 - c]).astype(jnp.int32)
    with jax.named_scope("terms_0"):
        terms = [walker_terms(place, pieces, walkers)]
    with jax.named_scope("branch"):
        branched = branch(plan, walkers, other_core, quarters)
    with jax.named_scope("core_gather_1"):
        mine[3] = after(mine[3], terms[0])
        pieces = mine + [to_other_core(p) for p in mine]
    with jax.named_scope("terms_1"):
        terms.append(walker_terms(place, pieces, walkers))
    with jax.named_scope("results"):
        bias = jnp.stack([t[:, :2] for t in terms], axis=1).reshape(slots, -1)
        energy = sum(t[:, 2:] for t in terms)
        others = [lax.ppermute(energy, "vec", ring(NY, k)) for k in range(1, NY)]
        energy = (energy + others[1]) + (others[0] + others[2])
        row = jnp.concatenate([bias, -0.5 * energy], axis=1)
        left = lax.ppermute(row, "walk", ring(size, 1))
        right = lax.ppermute(row, "walk", ring(size, -1))
        rows = jnp.concatenate([left, row, right], axis=0)
        chosen = jnp.sum(jnp.where((relative[:, None] == jnp.arange(3 * slots))[:, :, None], rows[None], 0.0), axis=1)
        force_bias = chosen[:, :-2].reshape(slots, len(terms), 2)
    return branched, force_bias, chosen[:, -2:]


def solution(mesh):
    return jax.shard_map(
        shards,
        mesh=mesh,
        in_specs=(P("walk", None, None), P("vec", "walk", None, None), P("vec", None), P("walk")),
        out_specs=(P("walk", None, None), P("walk", "vec", None), P("walk", None)),
        check_vma=False,
    )
```

```python
import jax
import jax.numpy as jnp
from jax import lax
from jax.experimental import pallas as pl
from jax.experimental.pallas import tpu as pltpu
from jax.sharding import PartitionSpec as P

NX, NZ, NC, NY = 4, 8, 2, 4


def walk_index(x, z, c):
    return ((x % NX) * NZ + z % NZ) * NC + c % NC


def chips():
    return [(x, z, c) for x in range(NX) for z in range(NZ) for c in range(NC)]


def to_chip(dx, dz):
    return [(walk_index(x, z, c), walk_index(x + (1 - 2 * c) * dx, z + (1 - 2 * c) * dz, c)) for x, z, c in chips()]


def ring(size, step):
    return [(i, (i + step) % size) for i in range(size)]


def across_chips():
    size = NX * NZ * NC
    return [(i, (i + 1) % size if i % NC == 1 else (i - 1) % size) for i in range(size)]


def terms_kernel(place_ref, *refs):
    pieces, (w_ref, out_ref, acc_ref, m_ref) = refs[:2 * NX], refs[2 * NX:]
    half, depth = pieces[0].shape
    electrons, orbitals = NC * half, 2 * depth
    for side in range(NC):
        acc_ref[...] = jnp.zeros_like(acc_ref)
        for k in range(NX):
            block = place_ref[side * NX + k]
            rows = pl.ds(pl.multiple_of(lax.rem(block, 2) * depth, depth), depth)
            acc_ref[lax.div(block, 2)] += jnp.dot(
                pieces[side * NX + k][...], w_ref[0, rows, :], preferred_element_type=jnp.float32
            )
        by_real, by_imag = acc_ref[0], acc_ref[1]
        place = pl.ds(pl.multiple_of(place_ref[NC * NX + side] * half, half), half)
        m_ref[0, place, :] = (by_real[:, :electrons] - by_imag[:, electrons:]).astype(jnp.bfloat16)
        m_ref[1, place, :] = (by_real[:, electrons:] + by_imag[:, :electrons]).astype(jnp.bfloat16)
    inverse = w_ref[0, orbitals:, :]
    g_by_real = jnp.dot(m_ref[0], inverse, preferred_element_type=jnp.float32)
    g_by_imag = jnp.dot(m_ref[1], inverse, preferred_element_type=jnp.float32)
    real = g_by_real[:, :electrons] - g_by_imag[:, electrons:]
    imag = g_by_real[:, electrons:] + g_by_imag[:, :electrons]
    real_t = real.T
    rows = lax.broadcasted_iota(jnp.int32, real.shape, 0)
    columns = lax.broadcasted_iota(jnp.int32, real.shape, 1)
    diagonal = rows == columns
    values = (
        jnp.sum(jnp.where(diagonal, real, 0.0)),
        jnp.sum(jnp.where(diagonal, imag, 0.0)),
        jnp.sum(real * real_t - imag * imag.T),
        2.0 * jnp.sum(imag * real_t),
    )
    lane = lax.broadcasted_iota(jnp.int32, out_ref.shape, 2)
    row = jnp.zeros(out_ref.shape, jnp.float32)
    for place, value in enumerate(values):
        row = jnp.where(lane == place, value, row)
    out_ref[...] = row


def walker_terms(place, pieces, walkers):
    count, height, width = walkers.shape
    half, depth = pieces[0].shape
    electrons = NC * half
    whole = pl.BlockSpec((half, depth), lambda i, _: (0, 0))
    out = pl.pallas_call(
        terms_kernel,
        grid_spec=pltpu.PrefetchScalarGridSpec(
            num_scalar_prefetch=1,
            grid=(count,),
            in_specs=[whole] * len(pieces) + [pl.BlockSpec((1, height, width), lambda i, _: (i, 0, 0))],
            out_specs=pl.BlockSpec((1, 8, 128), lambda i, _: (i, 0, 0)),
            scratch_shapes=[
                pltpu.VMEM((2, half, width), jnp.float32),
                pltpu.VMEM((2, electrons, width // 2), jnp.bfloat16),
            ],
        ),
        out_shape=jax.ShapeDtypeStruct((count, 8, 128), jnp.float32),
        compiler_params=pltpu.CompilerParams(vmem_limit_bytes=40 * 2**20),
        cost_estimate=pl.CostEstimate(
            flops=2 * count * electrons * (2 * NX * depth // 2 + width) * width,
            bytes_accessed=2 * (len(pieces) * pieces[0].size + walkers.size),
            transcendentals=0,
        ),
    )(place, *pieces, walkers)
    return out[:, 0, :4]


def branch_kernel(plan_ref, own_ref, core_ref, q0_ref, q1_ref, q2_ref, q3_ref, out_ref, held, in_sems, out_sems):
    slots, height, _ = out_ref.shape
    part = height // NY
    quarters = (q0_ref, q1_ref, q2_ref, q3_ref)

    def rows(k):
        return pl.ds(pl.multiple_of(plan_ref[2 * slots + k] * part, 16), part)

    def fetch(slot, k, source, index):
        src = (own_ref.at[index, rows(k)], core_ref.at[index, rows(k)], quarters[k].at[index])[source]
        return pltpu.make_async_copy(src, held.at[slot, k], in_sems.at[slot, k])

    def store(slot, k):
        return pltpu.make_async_copy(held.at[slot, k], out_ref.at[slot, rows(k)], out_sems.at[slot, k])

    for slot in range(slots):
        index = plan_ref[slots + slot]
        for source in range(3):
            @pl.when(plan_ref[slot] == source)
            def _(slot=slot, index=index, source=source):
                for k in range(NY):
                    fetch(slot, k, source, index).start()
    for slot in range(slots):
        for k in range(NY):
            fetch(slot, k, 0, 0).wait()
            store(slot, k).start()
    for slot in range(slots):
        for k in range(NY):
            store(slot, k).wait()


def branch(plan, own, other_core, quarters):
    anywhere = pl.BlockSpec(memory_space=pl.ANY)
    slots, height, width = own.shape
    return pl.pallas_call(
        branch_kernel,
        in_specs=[pl.BlockSpec(memory_space=pltpu.SMEM)] + [anywhere] * 6,
        out_specs=anywhere,
        out_shape=jax.ShapeDtypeStruct(own.shape, own.dtype),
        scratch_shapes=[
            pltpu.VMEM((slots, NY, height // NY, width), own.dtype),
            pltpu.SemaphoreType.DMA((slots, NY)),
            pltpu.SemaphoreType.DMA((slots, NY)),
        ],
        compiler_params=pltpu.CompilerParams(vmem_limit_bytes=16 * 2**20),
        cost_estimate=pl.CostEstimate(flops=0, bytes_accessed=4 * own.size, transcendentals=0),
    )(plan, own, other_core, *quarters)


def after(values, *done):
    return jax.tree.unflatten(
        jax.tree.structure(values), lax.optimization_barrier((*jax.tree.leaves(values), *done))[: len(jax.tree.leaves(values))]
    )


def cut_blocks(own, swapped, owner, x, c):
    electrons, columns = own.shape
    half, depth = electrons // NC, columns // NX

    def block(place):
        cut = [lax.dynamic_slice(a, (c * half, place * depth), (half, depth)) for a in (own, swapped)]
        return jnp.where(owner % NC == c, cut[0], cut[1])

    return [block((x + (1 - 2 * c) * dx + NX * NX) % NX) for dx in (0, 1, 3, 2)]


def scatter(blocks):
    return [lax.ppermute(sent, "walk", to_chip(dx, 0)) for dx, sent in zip((1, 3, 2), blocks[1:])]


def scattered(own, arrived, owner_x, x, c):
    for dx, block in zip((1, 3, 2), arrived):
        own = jnp.where((owner_x + (1 - 2 * c) * dx + NX * NX) % NX == x, block, own)
    return own


def flood_step(up, down):
    up, down = after((up, down))
    return lax.ppermute(up, "walk", to_chip(0, 1)), lax.ppermute(down, "walk", to_chip(0, -1))


def flooded(halves, streams, away):
    first, second = halves
    for step, (up, down) in enumerate(streams, 1):
        first = jnp.where(away == step, up, first)
        second = jnp.where(away == NZ - step, down, second)
        if step > 1:
            first = jnp.where(away == NZ - (step - 1), down, first)
            second = jnp.where(away == step - 1, up, second)
    return jnp.concatenate([first, second], axis=0)


def along_x(piece):
    return [lax.ppermute(piece, "walk", to_chip(dx, 0)) for dx in (1, 3, 2)]


def to_other_core(array):
    return lax.ppermute(array, "walk", [(i, i ^ 1) for i in range(NX * NZ * NC)])


def shards(walkers, chol, owners, branch_src):
    slots, height, _ = walkers.shape
    device, y = lax.axis_index("walk"), lax.axis_index("vec")
    x, z, c = device // (NZ * NC), device // NC % NZ, device % NC
    size = NX * NZ * NC
    total = slots * size
    own = chol[0, 0]
    owner = owners[0]
    both_ways = [
        (w * NY + v, w * NY + (v + (1 if w % NC == 0 else -1)) % NY) for w in range(size) for v in range(NY)
    ]

    def pass_on(quarter):
        return lax.ppermute(quarter, ("walk", "vec"), both_ways)

    with jax.named_scope("core_swap"):
        swapped = to_other_core(own)
    with jax.named_scope("halo_z"):
        part = height // NY
        quarter = lax.dynamic_slice_in_dim(walkers, y * part, part, 1)
        owner_x = [owner[g] // (NZ * NC) for g in range(2)]
        owner_z = [owner[g] // NC % NZ for g in range(2)]
        swapped, quarter, owner_x, owner_z = after((swapped, quarter, owner_x, owner_z))
        quarters = [lax.ppermute(quarter, "walk", across_chips())]
    with jax.named_scope("core_walkers"):
        other_core = to_other_core(after(walkers, swapped))
    with jax.named_scope("blocks"):
        blocks = [cut_blocks(own, swapped, owner[g], x, c) for g in range(2)]
    half = own.shape[0] // (2 * NC)
    is_owner = [owner_z[g] == z for g in range(2)]
    away = [((1 - 2 * c) * (z - owner_z[g]) + NZ) % NZ for g in range(2)]

    def turned(g, arrived):
        return [jnp.where(is_owner[g], halves[g][1 - i], arrived[i]) for i in range(2)]

    with jax.named_scope("x_scatter_0"):
        arrived = scatter(blocks[0])
        arrived, sent, quarters[0] = after((arrived, blocks[1], quarters[0]))
        piece = scattered(blocks[0][0], arrived, owner_x[0], x, c)
        halves = [(piece[:half], piece[half:])]
        halves[0], sent, quarters[0], other_core = after((halves[0], sent, quarters[0], other_core))
    with jax.named_scope("x_scatter_1"):
        arrived = scatter(sent)
    with jax.named_scope("z_flood"):
        first = flood_step(*halves[0])
    with jax.named_scope("halo_y"):
        quarters.append(pass_on(quarters[0]))
    with jax.named_scope("x_scatter_1"):
        arrived, first, quarters[1] = after((arrived, first, quarters[1]))
        piece = scattered(sent[0], arrived, owner_x[1], x, c)
        halves.append((piece[:half], piece[half:]))
    with jax.named_scope("z_flood"):
        ahead = turned(0, first)
        second = flood_step(*[jnp.stack([ahead[i], halves[1][i]]) for i in range(2)])
        late = is_owner[1] & (jnp.arange(2) == 1)[:, None, None]
        third = flood_step(*[jnp.where(late, halves[1][1 - i][None], second[i]) for i in range(2)])
    with jax.named_scope("halo_y"):
        quarters.append(pass_on(quarters[1]))
    with jax.named_scope("z_flood"):
        third, quarters[2] = after((third, quarters[2]))
        fourth = flood_step(*third)
    with jax.named_scope("halo_y"):
        quarters.append(pass_on(quarters[2]))
    with jax.named_scope("z_flood"):
        piece = flooded(halves[0], [first] + [[a[0] for a in b] for b in (second, third, fourth)], away[0])
        fifth = flood_step(*after([a[1] for a in fourth], piece))
    with jax.named_scope("x_gather_0"):
        mine = [piece] + along_x(piece)
    with jax.named_scope("z_flood"):
        piece = flooded(halves[1], [[a[1] for a in b] for b in (second, third, fourth)] + [fifth], away[1])
        piece, mine, quarters[3] = after((piece, mine, quarters[3]))
    with jax.named_scope("core_gather_0"):
        pieces = mine + [to_other_core(p) for p in mine]
        piece, pieces = after((piece, pieces))
    relative = (branch_src - (device - 1) * slots + total) % total
    side, index = relative // slots, relative % slots
    source = jnp.where(side == 1, 0, jnp.where((side == 0) == (c == 0), 2, 1))
    held = (y + jnp.arange(NY) * jnp.where(c == 0, NY - 1, 1)) % NY
    plan = after(jnp.concatenate([source, index, held]).astype(jnp.int32), pieces[-1])
    sign = 1 - 2 * c
    columns = [(x + k + NX) % NX for k in (0, -sign, sign, 2, 0, sign, -sign, 2)]
    place = jnp.stack([*columns, c, 1 - c]).astype(jnp.int32)
    with jax.named_scope("terms_0"):
        terms = [walker_terms(place, pieces, walkers)]
    with jax.named_scope("x_gather_1"):
        ahead = lax.ppermute(piece, "walk", to_chip(1, 0))
        later, ahead = after((piece, ahead), terms[0])
        mine = [piece, ahead, *[lax.ppermute(later, "walk", to_chip(dx, 0)) for dx in (3, 2)]]
    with jax.named_scope("branch"):
        branched = branch(plan, walkers, other_core, quarters)
    with jax.named_scope("core_gather_1"):
        mine[2] = after(mine[2], branched)
        pieces = mine + [to_other_core(p) for p in mine]
    with jax.named_scope("terms_1"):
        terms.append(walker_terms(place, pieces, walkers))
    with jax.named_scope("results"):
        bias = jnp.stack([t[:, :2] for t in terms], axis=1).reshape(slots, -1)
        energy = sum(t[:, 2:] for t in terms)
        others = [lax.ppermute(energy, "vec", ring(NY, k)) for k in range(1, NY)]
        energy = (energy + others[1]) + (others[0] + others[2])
        row = jnp.concatenate([bias, -0.5 * energy], axis=1)
        left = lax.ppermute(row, "walk", ring(size, 1))
        right = lax.ppermute(row, "walk", ring(size, -1))
        rows = jnp.concatenate([left, row, right], axis=0)
        chosen = jnp.sum(jnp.where((relative[:, None] == jnp.arange(3 * slots))[:, :, None], rows[None], 0.0), axis=1)
        force_bias = chosen[:, :-2].reshape(slots, len(terms), 2)
    return branched, force_bias, chosen[:, -2:]


def solution(mesh):
    return jax.shard_map(
        shards,
        mesh=mesh,
        in_specs=(P("walk", None, None), P("vec", "walk", None, None), P("vec", None), P("walk")),
        out_specs=(P("walk", None, None), P("walk", "vec", None), P("walk", None)),
        check_vma=False,
    )
```

```python
import jax
import jax.numpy as jnp
from jax import lax
from jax.experimental import pallas as pl
from jax.experimental.pallas import tpu as pltpu
from jax.sharding import PartitionSpec as P

NX, NZ, NC, NY = 4, 8, 2, 4


def walk_index(x, z, c):
    return ((x % NX) * NZ + z % NZ) * NC + c % NC


def chips():
    return [(x, z, c) for x in range(NX) for z in range(NZ) for c in range(NC)]


def to_chip(dx, dz):
    return [(walk_index(x, z, c), walk_index(x + (1 - 2 * c) * dx, z + (1 - 2 * c) * dz, c)) for x, z, c in chips()]


def ring(size, step):
    return [(i, (i + step) % size) for i in range(size)]


def across_chips():
    size = NX * NZ * NC
    return [(i, (i + 1) % size if i % NC == 1 else (i - 1) % size) for i in range(size)]


def terms_kernel(place_ref, *refs):
    pieces, (w_ref, out_ref, acc_ref, m_ref) = refs[:2 * NX], refs[2 * NX:]
    half, depth = pieces[0].shape
    electrons, orbitals = NC * half, 2 * depth
    for side in range(NC):
        acc_ref[...] = jnp.zeros_like(acc_ref)
        for k in range(NX):
            block = place_ref[side * NX + k]
            rows = pl.ds(pl.multiple_of(lax.rem(block, 2) * depth, depth), depth)
            acc_ref[lax.div(block, 2)] += jnp.dot(
                pieces[side * NX + k][...], w_ref[0, rows, :], preferred_element_type=jnp.float32
            )
        by_real, by_imag = acc_ref[0], acc_ref[1]
        place = pl.ds(pl.multiple_of(place_ref[NC * NX + side] * half, half), half)
        m_ref[0, place, :] = (by_real[:, :electrons] - by_imag[:, electrons:]).astype(jnp.bfloat16)
        m_ref[1, place, :] = (by_real[:, electrons:] + by_imag[:, :electrons]).astype(jnp.bfloat16)
    inverse = w_ref[0, orbitals:, :]
    g_by_real = jnp.dot(m_ref[0], inverse, preferred_element_type=jnp.float32)
    g_by_imag = jnp.dot(m_ref[1], inverse, preferred_element_type=jnp.float32)
    real = g_by_real[:, :electrons] - g_by_imag[:, electrons:]
    imag = g_by_real[:, electrons:] + g_by_imag[:, :electrons]
    real_t = real.T
    rows = lax.broadcasted_iota(jnp.int32, real.shape, 0)
    columns = lax.broadcasted_iota(jnp.int32, real.shape, 1)
    diagonal = rows == columns
    values = (
        jnp.sum(jnp.where(diagonal, real, 0.0)),
        jnp.sum(jnp.where(diagonal, imag, 0.0)),
        jnp.sum(real * real_t - imag * imag.T),
        2.0 * jnp.sum(imag * real_t),
    )
    lane = lax.broadcasted_iota(jnp.int32, out_ref.shape, 2)
    row = jnp.zeros(out_ref.shape, jnp.float32)
    for place, value in enumerate(values):
        row = jnp.where(lane == place, value, row)
    out_ref[...] = row


def walker_terms(place, pieces, walkers):
    count, height, width = walkers.shape
    half, depth = pieces[0].shape
    electrons = NC * half
    whole = pl.BlockSpec((half, depth), lambda i, _: (0, 0))
    out = pl.pallas_call(
        terms_kernel,
        grid_spec=pltpu.PrefetchScalarGridSpec(
            num_scalar_prefetch=1,
            grid=(count,),
            in_specs=[whole] * len(pieces) + [pl.BlockSpec((1, height, width), lambda i, _: (i, 0, 0))],
            out_specs=pl.BlockSpec((1, 8, 128), lambda i, _: (i, 0, 0)),
            scratch_shapes=[
                pltpu.VMEM((2, half, width), jnp.float32),
                pltpu.VMEM((2, electrons, width // 2), jnp.bfloat16),
            ],
        ),
        out_shape=jax.ShapeDtypeStruct((count, 8, 128), jnp.float32),
        compiler_params=pltpu.CompilerParams(vmem_limit_bytes=50 * 2**20),
        cost_estimate=pl.CostEstimate(
            flops=2 * count * electrons * (2 * NX * depth // 2 + width) * width,
            bytes_accessed=2 * (len(pieces) * pieces[0].size + walkers.size),
            transcendentals=0,
        ),
    )(place, *pieces, walkers)
    return out[:, 0, :4]


def branch_kernel(plan_ref, own_ref, core_ref, q0_ref, q1_ref, q2_ref, q3_ref, out_ref, held, in_sems, out_sems):
    slots, height, _ = out_ref.shape
    part = height // NY
    quarters = (q0_ref, q1_ref, q2_ref, q3_ref)

    def rows(k):
        return pl.ds(pl.multiple_of(plan_ref[2 * slots + k] * part, 16), part)

    def fetch(slot, k, source, index):
        src = (own_ref.at[index, rows(k)], core_ref.at[index, rows(k)], quarters[k].at[index])[source]
        return pltpu.make_async_copy(src, held.at[slot, k], in_sems.at[slot, k])

    def store(slot, k):
        return pltpu.make_async_copy(held.at[slot, k], out_ref.at[slot, rows(k)], out_sems.at[slot, k])

    for slot in range(slots):
        index = plan_ref[slots + slot]
        for source in range(3):
            @pl.when(plan_ref[slot] == source)
            def _(slot=slot, index=index, source=source):
                for k in range(NY):
                    fetch(slot, k, source, index).start()
    for slot in range(slots):
        for k in range(NY):
            fetch(slot, k, 0, 0).wait()
            store(slot, k).start()
    for slot in range(slots):
        for k in range(NY):
            store(slot, k).wait()


def branch(plan, own, other_core, quarters):
    anywhere = pl.BlockSpec(memory_space=pl.ANY)
    slots, height, width = own.shape
    return pl.pallas_call(
        branch_kernel,
        in_specs=[pl.BlockSpec(memory_space=pltpu.SMEM)] + [anywhere] * 6,
        out_specs=anywhere,
        out_shape=jax.ShapeDtypeStruct(own.shape, own.dtype),
        scratch_shapes=[
            pltpu.VMEM((slots, NY, height // NY, width), own.dtype),
            pltpu.SemaphoreType.DMA((slots, NY)),
            pltpu.SemaphoreType.DMA((slots, NY)),
        ],
        compiler_params=pltpu.CompilerParams(vmem_limit_bytes=16 * 2**20),
        cost_estimate=pl.CostEstimate(flops=0, bytes_accessed=4 * own.size, transcendentals=0),
    )(plan, own, other_core, *quarters)


def after(values, *done):
    return jax.tree.unflatten(
        jax.tree.structure(values), lax.optimization_barrier((*jax.tree.leaves(values), *done))[: len(jax.tree.leaves(values))]
    )


def cut_blocks(own, swapped, owner, x, c):
    electrons, columns = own.shape
    half, depth = electrons // NC, columns // NX

    def block(place):
        cut = [lax.dynamic_slice(a, (c * half, place * depth), (half, depth)) for a in (own, swapped)]
        return jnp.where(owner % NC == c, cut[0], cut[1])

    return [block((x + (1 - 2 * c) * dx + NX * NX) % NX) for dx in (0, 1, 3, 2)]


def scatter(blocks):
    return [lax.ppermute(sent, "walk", to_chip(dx, 0)) for dx, sent in zip((1, 3, 2), blocks[1:])]


def scattered(own, arrived, owner_x, x, c):
    for dx, block in zip((1, 3, 2), arrived):
        own = jnp.where((owner_x + (1 - 2 * c) * dx + NX * NX) % NX == x, block, own)
    return own


def flood_step(up, down):
    up, down = after((up, down))
    return lax.ppermute(up, "walk", to_chip(0, 1)), lax.ppermute(down, "walk", to_chip(0, -1))


def flooded(halves, streams, away):
    first, second = halves
    for step, (up, down) in enumerate(streams, 1):
        first = jnp.where(away == step, up, first)
        second = jnp.where(away == NZ - step, down, second)
        if step > 1:
            first = jnp.where(away == NZ - (step - 1), down, first)
            second = jnp.where(away == step - 1, up, second)
    return jnp.concatenate([first, second], axis=0)


def along_x(piece):
    return [lax.ppermute(piece, "walk", to_chip(dx, 0)) for dx in (1, 3, 2)]


def to_other_core(array):
    return lax.ppermute(array, "walk", [(i, i ^ 1) for i in range(NX * NZ * NC)])


def shards(walkers, chol, owners, branch_src):
    slots, height, _ = walkers.shape
    device, y = lax.axis_index("walk"), lax.axis_index("vec")
    x, z, c = device // (NZ * NC), device // NC % NZ, device % NC
    size = NX * NZ * NC
    total = slots * size
    own = chol[0, 0]
    owner = owners[0]
    both_ways = [
        (w * NY + v, w * NY + (v + (1 if w % NC == 0 else -1)) % NY) for w in range(size) for v in range(NY)
    ]

    def pass_on(quarter):
        return lax.ppermute(quarter, ("walk", "vec"), both_ways)

    with jax.named_scope("core_swap"):
        swapped = to_other_core(own)
    with jax.named_scope("halo_z"):
        part = height // NY
        quarter = lax.dynamic_slice_in_dim(walkers, y * part, part, 1)
        owner_x = [owner[g] // (NZ * NC) for g in range(2)]
        owner_z = [owner[g] // NC % NZ for g in range(2)]
        swapped, quarter, owner_x, owner_z = after((swapped, quarter, owner_x, owner_z))
        quarters = [lax.ppermute(quarter, "walk", across_chips())]
    with jax.named_scope("core_walkers"):
        other_core = to_other_core(after(walkers, swapped))
    with jax.named_scope("blocks"):
        blocks = [cut_blocks(own, swapped, owner[g], x, c) for g in range(2)]
    half = own.shape[0] // (2 * NC)
    is_owner = [owner_z[g] == z for g in range(2)]
    away = [((1 - 2 * c) * (z - owner_z[g]) + NZ) % NZ for g in range(2)]

    def turned(g, arrived):
        return [jnp.where(is_owner[g], halves[g][1 - i], arrived[i]) for i in range(2)]

    with jax.named_scope("x_scatter_0"):
        arrived = scatter(blocks[0])
        arrived, sent, quarters[0] = after((arrived[::-1], blocks[1], quarters[0]))
        arrived = arrived[::-1]
        piece = scattered(blocks[0][0], arrived, owner_x[0], x, c)
        halves = [(piece[:half], piece[half:])]
        halves[0], sent, quarters[0], other_core = after((halves[0], sent, quarters[0], other_core))
    with jax.named_scope("x_scatter_1"):
        arrived = scatter(sent)
    with jax.named_scope("z_flood"):
        first = flood_step(*halves[0])
    with jax.named_scope("halo_y"):
        quarters.append(pass_on(quarters[0]))
    with jax.named_scope("x_scatter_1"):
        arrived, first, quarters[1] = after((arrived, first, quarters[1]))
        piece = scattered(sent[0], arrived, owner_x[1], x, c)
        halves.append((piece[:half], piece[half:]))
    with jax.named_scope("z_flood"):
        ahead = turned(0, first)
        second = flood_step(*[jnp.stack([ahead[i], halves[1][i]]) for i in range(2)])
        late = is_owner[1] & (jnp.arange(2) == 1)[:, None, None]
        third = flood_step(*[jnp.where(late, halves[1][1 - i][None], second[i]) for i in range(2)])
    with jax.named_scope("halo_y"):
        quarters.append(pass_on(quarters[1]))
    with jax.named_scope("z_flood"):
        third, quarters[2] = after((third, quarters[2]))
        fourth = flood_step(*third)
    with jax.named_scope("halo_y"):
        quarters.append(pass_on(quarters[2]))
    with jax.named_scope("z_flood"):
        piece = flooded(halves[0], [first] + [[a[0] for a in b] for b in (second, third, fourth)], away[0])
        fifth = flood_step(*after([a[1] for a in fourth], piece))
    with jax.named_scope("x_gather_0"):
        mine = [piece] + along_x(piece)
    with jax.named_scope("z_flood"):
        piece = flooded(halves[1], [[a[1] for a in b] for b in (second, third, fourth)] + [fifth], away[1])
        piece, mine, quarters[3] = after((piece, mine[::-1], quarters[3]))
        mine = mine[::-1]
    with jax.named_scope("core_gather_0"):
        pieces = mine + [to_other_core(p) for p in mine]
        piece, pieces = after((piece, pieces))
    relative = (branch_src - (device - 1) * slots + total) % total
    side, index = relative // slots, relative % slots
    source = jnp.where(side == 1, 0, jnp.where((side == 0) == (c == 0), 2, 1))
    held = (y + jnp.arange(NY) * jnp.where(c == 0, NY - 1, 1)) % NY
    plan = after(jnp.concatenate([source, index, held]).astype(jnp.int32), pieces[-1])
    sign = 1 - 2 * c
    columns = [(x + k + NX) % NX for k in (0, -sign, sign, 2, 0, sign, -sign, 2)]
    place = jnp.stack([*columns, c, 1 - c]).astype(jnp.int32)
    with jax.named_scope("terms_0"):
        terms = [walker_terms(place, pieces, walkers)]
    with jax.named_scope("x_gather_1"):
        ahead = lax.ppermute(piece, "walk", to_chip(1, 0))
        later, ahead = after((piece, ahead), terms[0])
        mine = [piece, ahead, *[lax.ppermute(later, "walk", to_chip(dx, 0)) for dx in (3, 2)]]
    with jax.named_scope("branch"):
        branched = branch(plan, walkers, other_core, quarters)
    with jax.named_scope("core_gather_1"):
        mine[2] = after(mine[2], branched)
        pieces = mine + [to_other_core(p) for p in mine]
    with jax.named_scope("terms_1"):
        terms.append(walker_terms(place, pieces, walkers))
    with jax.named_scope("results"):
        bias = jnp.stack([t[:, :2] for t in terms], axis=1).reshape(slots, -1)
        energy = sum(t[:, 2:] for t in terms)
        others = [lax.ppermute(energy, "vec", ring(NY, k)) for k in range(1, NY)]
        energy = (energy + others[1]) + (others[0] + others[2])
        row = jnp.concatenate([bias, -0.5 * energy], axis=1)
        left = lax.ppermute(row, "walk", ring(size, 1))
        right = lax.ppermute(row, "walk", ring(size, -1))
        rows = jnp.concatenate([left, row, right], axis=0)
        chosen = jnp.sum(jnp.where((relative[:, None] == jnp.arange(3 * slots))[:, :, None], rows[None], 0.0), axis=1)
        force_bias = chosen[:, :-2].reshape(slots, len(terms), 2)
    return branched, force_bias, chosen[:, -2:]


def solution(mesh):
    return jax.shard_map(
        shards,
        mesh=mesh,
        in_specs=(P("walk", None, None), P("vec", "walk", None, None), P("vec", None), P("walk")),
        out_specs=(P("walk", None, None), P("walk", "vec", None), P("walk", None)),
        check_vma=False,
    )
```

```python
import jax
import jax.numpy as jnp
from jax import lax
from jax.experimental import pallas as pl
from jax.experimental.pallas import tpu as pltpu
from jax.sharding import PartitionSpec as P

NX, NZ, NC, NY = 4, 8, 2, 4


def walk_index(x, z, c):
    return ((x % NX) * NZ + z % NZ) * NC + c % NC


def chips():
    return [(x, z, c) for x in range(NX) for z in range(NZ) for c in range(NC)]


def to_chip(dx, dz):
    return [(walk_index(x, z, c), walk_index(x + (1 - 2 * c) * dx, z + (1 - 2 * c) * dz, c)) for x, z, c in chips()]


def ring(size, step):
    return [(i, (i + step) % size) for i in range(size)]


def across_chips():
    size = NX * NZ * NC
    return [(i, (i + 1) % size if i % NC == 1 else (i - 1) % size) for i in range(size)]


def terms_kernel(place_ref, *refs):
    pieces, (w_ref, out_ref, acc_ref, m_ref) = refs[:2 * NX], refs[2 * NX:]
    half, depth = pieces[0].shape
    electrons, orbitals = NC * half, 2 * depth
    for side in range(NC):
        acc_ref[...] = jnp.zeros_like(acc_ref)
        for k in range(NX):
            block = place_ref[side * NX + k]
            rows = pl.ds(pl.multiple_of(lax.rem(block, 2) * depth, depth), depth)
            acc_ref[lax.div(block, 2)] += jnp.dot(
                pieces[side * NX + k][...], w_ref[0, rows, :], preferred_element_type=jnp.float32
            )
        by_real, by_imag = acc_ref[0], acc_ref[1]
        place = pl.ds(pl.multiple_of(place_ref[NC * NX + side] * half, half), half)
        m_ref[0, place, :] = (by_real[:, :electrons] - by_imag[:, electrons:]).astype(jnp.bfloat16)
        m_ref[1, place, :] = (by_real[:, electrons:] + by_imag[:, :electrons]).astype(jnp.bfloat16)
    inverse = w_ref[0, orbitals:, :]
    g_by_real = jnp.dot(m_ref[0], inverse, preferred_element_type=jnp.float32)
    g_by_imag = jnp.dot(m_ref[1], inverse, preferred_element_type=jnp.float32)
    real = g_by_real[:, :electrons] - g_by_imag[:, electrons:]
    imag = g_by_real[:, electrons:] + g_by_imag[:, :electrons]
    real_t = real.T
    rows = lax.broadcasted_iota(jnp.int32, real.shape, 0)
    columns = lax.broadcasted_iota(jnp.int32, real.shape, 1)
    diagonal = rows == columns
    values = (
        jnp.sum(jnp.where(diagonal, real, 0.0)),
        jnp.sum(jnp.where(diagonal, imag, 0.0)),
        jnp.sum(real * real_t - imag * imag.T),
        2.0 * jnp.sum(imag * real_t),
    )
    lane = lax.broadcasted_iota(jnp.int32, out_ref.shape, 2)
    row = jnp.zeros(out_ref.shape, jnp.float32)
    for place, value in enumerate(values):
        row = jnp.where(lane == place, value, row)
    out_ref[...] = row


def walker_terms(place, pieces, walkers):
    count, height, width = walkers.shape
    half, depth = pieces[0].shape
    electrons = NC * half
    whole = pl.BlockSpec((half, depth), lambda i, _: (0, 0))
    out = pl.pallas_call(
        terms_kernel,
        grid_spec=pltpu.PrefetchScalarGridSpec(
            num_scalar_prefetch=1,
            grid=(count,),
            in_specs=[whole] * len(pieces) + [pl.BlockSpec((1, height, width), lambda i, _: (i, 0, 0))],
            out_specs=pl.BlockSpec((1, 8, 128), lambda i, _: (i, 0, 0)),
            scratch_shapes=[
                pltpu.VMEM((2, half, width), jnp.float32),
                pltpu.VMEM((2, electrons, width // 2), jnp.bfloat16),
            ],
        ),
        out_shape=jax.ShapeDtypeStruct((count, 8, 128), jnp.float32),
        compiler_params=pltpu.CompilerParams(vmem_limit_bytes=40 * 2**20),
        cost_estimate=pl.CostEstimate(
            flops=2 * count * electrons * (2 * NX * depth // 2 + width) * width,
            bytes_accessed=2 * (len(pieces) * pieces[0].size + walkers.size),
            transcendentals=0,
        ),
    )(place, *pieces, walkers)
    return out[:, 0, :4]


def branch_kernel(plan_ref, own_ref, core_ref, q0_ref, q1_ref, q2_ref, q3_ref, out_ref, held, in_sems, out_sems):
    slots, height, _ = out_ref.shape
    part = height // NY
    quarters = (q0_ref, q1_ref, q2_ref, q3_ref)

    def rows(k):
        return pl.ds(pl.multiple_of(plan_ref[2 * slots + k] * part, 16), part)

    def fetch(slot, k, source, index):
        src = (own_ref.at[index, rows(k)], core_ref.at[index, rows(k)], quarters[k].at[index])[source]
        return pltpu.make_async_copy(src, held.at[slot, k], in_sems.at[slot, k])

    def store(slot, k):
        return pltpu.make_async_copy(held.at[slot, k], out_ref.at[slot, rows(k)], out_sems.at[slot, k])

    for slot in range(slots):
        index = plan_ref[slots + slot]
        for source in range(3):
            @pl.when(plan_ref[slot] == source)
            def _(slot=slot, index=index, source=source):
                for k in range(NY):
                    fetch(slot, k, source, index).start()
    for slot in range(slots):
        for k in range(NY):
            fetch(slot, k, 0, 0).wait()
            store(slot, k).start()
    for slot in range(slots):
        for k in range(NY):
            store(slot, k).wait()


def branch(plan, own, other_core, quarters):
    anywhere = pl.BlockSpec(memory_space=pl.ANY)
    slots, height, width = own.shape
    return pl.pallas_call(
        branch_kernel,
        in_specs=[pl.BlockSpec(memory_space=pltpu.SMEM)] + [anywhere] * 6,
        out_specs=anywhere,
        out_shape=jax.ShapeDtypeStruct(own.shape, own.dtype),
        scratch_shapes=[
            pltpu.VMEM((slots, NY, height // NY, width), own.dtype),
            pltpu.SemaphoreType.DMA((slots, NY)),
            pltpu.SemaphoreType.DMA((slots, NY)),
        ],
        compiler_params=pltpu.CompilerParams(vmem_limit_bytes=50 * 2**20),
        cost_estimate=pl.CostEstimate(flops=0, bytes_accessed=4 * own.size, transcendentals=0),
    )(plan, own, other_core, *quarters)


def after(values, *done):
    return jax.tree.unflatten(
        jax.tree.structure(values), lax.optimization_barrier((*jax.tree.leaves(values), *done))[: len(jax.tree.leaves(values))]
    )


def cut_blocks(own, swapped, owner, x, c):
    electrons, columns = own.shape
    half, depth = electrons // NC, columns // NX

    def block(place):
        cut = [lax.dynamic_slice(a, (c * half, place * depth), (half, depth)) for a in (own, swapped)]
        return jnp.where(owner % NC == c, cut[0], cut[1])

    return [block((x + (1 - 2 * c) * dx + NX * NX) % NX) for dx in (0, 1, 3, 2)]


def scatter(blocks):
    return [lax.ppermute(sent, "walk", to_chip(dx, 0)) for dx, sent in zip((1, 3, 2), blocks[1:])]


def scattered(own, arrived, owner_x, x, c):
    for dx, block in zip((1, 3, 2), arrived):
        own = jnp.where((owner_x + (1 - 2 * c) * dx + NX * NX) % NX == x, block, own)
    return own


def flood_step(up, down):
    up, down = after((up, down))
    return lax.ppermute(up, "walk", to_chip(0, 1)), lax.ppermute(down, "walk", to_chip(0, -1))


def flooded(halves, streams, away):
    first, second = halves
    for step, (up, down) in enumerate(streams, 1):
        first = jnp.where(away == step, up, first)
        second = jnp.where(away == NZ - step, down, second)
        if step > 1:
            first = jnp.where(away == NZ - (step - 1), down, first)
            second = jnp.where(away == step - 1, up, second)
    return jnp.concatenate([first, second], axis=0)


def along_x(piece):
    return [lax.ppermute(piece, "walk", to_chip(dx, 0)) for dx in (1, 3, 2)]


def to_other_core(array):
    return lax.ppermute(array, "walk", [(i, i ^ 1) for i in range(NX * NZ * NC)])


def shards(walkers, chol, owners, branch_src):
    slots, height, _ = walkers.shape
    device, y = lax.axis_index("walk"), lax.axis_index("vec")
    x, z, c = device // (NZ * NC), device // NC % NZ, device % NC
    size = NX * NZ * NC
    total = slots * size
    own = chol[0, 0]
    owner = owners[0]
    both_ways = [
        (w * NY + v, w * NY + (v + (1 if w % NC == 0 else -1)) % NY) for w in range(size) for v in range(NY)
    ]

    def pass_on(quarter):
        return lax.ppermute(quarter, ("walk", "vec"), both_ways)

    with jax.named_scope("core_swap"):
        swapped = to_other_core(own)
    with jax.named_scope("halo_z"):
        part = height // NY
        quarter = lax.dynamic_slice_in_dim(walkers, y * part, part, 1)
        owner_x = [owner[g] // (NZ * NC) for g in range(2)]
        owner_z = [owner[g] // NC % NZ for g in range(2)]
        swapped, quarter, owner_x, owner_z = after((swapped, quarter, owner_x, owner_z))
        quarters = [lax.ppermute(quarter, "walk", across_chips())]
    with jax.named_scope("core_walkers"):
        other_core = to_other_core(after(walkers, swapped))
    with jax.named_scope("blocks"):
        blocks = [cut_blocks(own, swapped, owner[g], x, c) for g in range(2)]
    half = own.shape[0] // (2 * NC)
    is_owner = [owner_z[g] == z for g in range(2)]
    away = [((1 - 2 * c) * (z - owner_z[g]) + NZ) % NZ for g in range(2)]

    def turned(g, arrived):
        return [jnp.where(is_owner[g], halves[g][1 - i], arrived[i]) for i in range(2)]

    with jax.named_scope("x_scatter_0"):
        arrived = scatter(blocks[0])
        arrived, sent, quarters[0] = after((arrived[::-1], blocks[1], quarters[0]))
        arrived = arrived[::-1]
        piece = scattered(blocks[0][0], arrived, owner_x[0], x, c)
        halves = [(piece[:half], piece[half:])]
        halves[0], sent, quarters[0], other_core = after((halves[0], sent, quarters[0], other_core))
    with jax.named_scope("x_scatter_1"):
        arrived = scatter(sent)
    with jax.named_scope("z_flood"):
        first = flood_step(*halves[0])
    with jax.named_scope("halo_y"):
        quarters.append(pass_on(quarters[0]))
    with jax.named_scope("x_scatter_1"):
        arrived, first, quarters[1] = after((arrived, first, quarters[1]))
        piece = scattered(sent[0], arrived, owner_x[1], x, c)
        halves.append((piece[:half], piece[half:]))
    with jax.named_scope("z_flood"):
        ahead = turned(0, first)
        second = flood_step(*[jnp.stack([ahead[i], halves[1][i]]) for i in range(2)])
        late = is_owner[1] & (jnp.arange(2) == 1)[:, None, None]
        third = flood_step(*[jnp.where(late, halves[1][1 - i][None], second[i]) for i in range(2)])
    with jax.named_scope("halo_y"):
        quarters.append(pass_on(quarters[1]))
    with jax.named_scope("z_flood"):
        third, quarters[2] = after((third, quarters[2]))
        fourth = flood_step(*third)
    with jax.named_scope("halo_y"):
        quarters.append(pass_on(quarters[2]))
    with jax.named_scope("z_flood"):
        piece = flooded(halves[0], [first] + [[a[0] for a in b] for b in (second, third, fourth)], away[0])
        fifth = flood_step(*after([a[1] for a in fourth], piece))
    with jax.named_scope("x_gather_0"):
        mine = [piece] + along_x(piece)
    with jax.named_scope("z_flood"):
        piece = flooded(halves[1], [[a[1] for a in b] for b in (second, third, fourth)] + [fifth], away[1])
        piece, mine, quarters[3] = after((piece, mine[::-1], quarters[3]))
        mine = mine[::-1]
    with jax.named_scope("core_gather_0"):
        pieces = mine + [to_other_core(p) for p in mine]
        piece, pieces = after((piece, pieces))
    relative = (branch_src - (device - 1) * slots + total) % total
    side, index = relative // slots, relative % slots
    source = jnp.where(side == 1, 0, jnp.where((side == 0) == (c == 0), 2, 1))
    held = (y + jnp.arange(NY) * jnp.where(c == 0, NY - 1, 1)) % NY
    plan = after(jnp.concatenate([source, index, held]).astype(jnp.int32), pieces[-1])
    sign = 1 - 2 * c
    columns = [(x + k + NX) % NX for k in (0, -sign, sign, 2, 0, sign, -sign, 2)]
    place = jnp.stack([*columns, c, 1 - c]).astype(jnp.int32)
    with jax.named_scope("branch"):
        branched = branch(plan, walkers, other_core, quarters)
    with jax.named_scope("x_gather_1"):
        ahead = lax.ppermute(piece, "walk", to_chip(1, 0))
        later, ahead, branched = after((piece, ahead, branched))
        mine = [piece, ahead, *[lax.ppermute(later, "walk", to_chip(dx, 0)) for dx in (3, 2)]]
    with jax.named_scope("terms_0"):
        terms = [walker_terms(place, pieces, walkers)]
    with jax.named_scope("core_gather_1"):
        mine[2] = after(mine[2], terms[0])
        pieces = mine + [to_other_core(p) for p in mine]
    with jax.named_scope("terms_1"):
        terms.append(walker_terms(place, pieces, walkers))
    with jax.named_scope("results"):
        bias = jnp.stack([t[:, :2] for t in terms], axis=1).reshape(slots, -1)
        energy = sum(t[:, 2:] for t in terms)
        others = [lax.ppermute(energy, "vec", ring(NY, k)) for k in range(1, NY)]
        energy = (energy + others[1]) + (others[0] + others[2])
        row = jnp.concatenate([bias, -0.5 * energy], axis=1)
        left = lax.ppermute(row, "walk", ring(size, 1))
        right = lax.ppermute(row, "walk", ring(size, -1))
        rows = jnp.concatenate([left, row, right], axis=0)
        chosen = jnp.sum(jnp.where((relative[:, None] == jnp.arange(3 * slots))[:, :, None], rows[None], 0.0), axis=1)
        force_bias = chosen[:, :-2].reshape(slots, len(terms), 2)
    return branched, force_bias, chosen[:, -2:]


def solution(mesh):
    return jax.shard_map(
        shards,
        mesh=mesh,
        in_specs=(P("walk", None, None), P("vec", "walk", None, None), P("vec", None), P("walk")),
        out_specs=(P("walk", None, None), P("walk", "vec", None), P("walk", None)),
        check_vma=False,
    )
```

```python
import jax
import jax.numpy as jnp
from jax import lax
from jax.experimental import pallas as pl
from jax.experimental.pallas import tpu as pltpu
from jax.sharding import PartitionSpec as P

NX, NZ, NC, NY = 4, 8, 2, 4


def walk_index(x, z, c):
    return ((x % NX) * NZ + z % NZ) * NC + c % NC


def chips():
    return [(x, z, c) for x in range(NX) for z in range(NZ) for c in range(NC)]


def to_chip(dx, dz):
    return [(walk_index(x, z, c), walk_index(x + (1 - 2 * c) * dx, z + (1 - 2 * c) * dz, c)) for x, z, c in chips()]


def ring(size, step):
    return [(i, (i + step) % size) for i in range(size)]


def across_chips():
    size = NX * NZ * NC
    return [(i, (i + 1) % size if i % NC == 1 else (i - 1) % size) for i in range(size)]


def terms_kernel(place_ref, *refs):
    pieces, (w_ref, out_ref, acc_ref, m_ref) = refs[:2 * NX], refs[2 * NX:]
    half, depth = pieces[0].shape
    electrons, orbitals = NC * half, 2 * depth
    for side in range(NC):
        acc_ref[...] = jnp.zeros_like(acc_ref)
        for k in range(NX):
            block = place_ref[side * NX + k]
            rows = pl.ds(pl.multiple_of(lax.rem(block, 2) * depth, depth), depth)
            acc_ref[lax.div(block, 2)] += jnp.dot(
                pieces[side * NX + k][...], w_ref[0, rows, :], preferred_element_type=jnp.float32
            )
        by_real, by_imag = acc_ref[0], acc_ref[1]
        place = pl.ds(pl.multiple_of(place_ref[NC * NX + side] * half, half), half)
        m_ref[0, place, :] = (by_real[:, :electrons] - by_imag[:, electrons:]).astype(jnp.bfloat16)
        m_ref[1, place, :] = (by_real[:, electrons:] + by_imag[:, :electrons]).astype(jnp.bfloat16)
    inverse = w_ref[0, orbitals:, :]
    g_by_real = jnp.dot(m_ref[0], inverse, preferred_element_type=jnp.float32)
    g_by_imag = jnp.dot(m_ref[1], inverse, preferred_element_type=jnp.float32)
    real = g_by_real[:, :electrons] - g_by_imag[:, electrons:]
    imag = g_by_real[:, electrons:] + g_by_imag[:, :electrons]
    real_t = real.T
    rows = lax.broadcasted_iota(jnp.int32, real.shape, 0)
    columns = lax.broadcasted_iota(jnp.int32, real.shape, 1)
    diagonal = rows == columns
    values = (
        jnp.sum(jnp.where(diagonal, real, 0.0)),
        jnp.sum(jnp.where(diagonal, imag, 0.0)),
        jnp.sum(real * real_t - imag * imag.T),
        2.0 * jnp.sum(imag * real_t),
    )
    lane = lax.broadcasted_iota(jnp.int32, out_ref.shape, 2)
    row = jnp.zeros(out_ref.shape, jnp.float32)
    for place, value in enumerate(values):
        row = jnp.where(lane == place, value, row)
    out_ref[...] = row


def walker_terms(place, pieces, walkers):
    count, height, width = walkers.shape
    half, depth = pieces[0].shape
    electrons = NC * half
    whole = pl.BlockSpec((half, depth), lambda i, _: (0, 0))
    out = pl.pallas_call(
        terms_kernel,
        grid_spec=pltpu.PrefetchScalarGridSpec(
            num_scalar_prefetch=1,
            grid=(count,),
            in_specs=[whole] * len(pieces) + [pl.BlockSpec((1, height, width), lambda i, _: (i, 0, 0))],
            out_specs=pl.BlockSpec((1, 8, 128), lambda i, _: (i, 0, 0)),
            scratch_shapes=[
                pltpu.VMEM((2, half, width), jnp.float32),
                pltpu.VMEM((2, electrons, width // 2), jnp.bfloat16),
            ],
        ),
        out_shape=jax.ShapeDtypeStruct((count, 8, 128), jnp.float32),
        compiler_params=pltpu.CompilerParams(vmem_limit_bytes=40 * 2**20),
        cost_estimate=pl.CostEstimate(
            flops=2 * count * electrons * (2 * NX * depth // 2 + width) * width,
            bytes_accessed=2 * (len(pieces) * pieces[0].size + walkers.size),
            transcendentals=0,
        ),
    )(place, *pieces, walkers)
    return out[:, 0, :4]


def branch_kernel(plan_ref, own_ref, core_ref, q0_ref, q1_ref, q2_ref, q3_ref, out_ref, held, in_sems, out_sems):
    slots, height, _ = out_ref.shape
    part = height // NY
    quarters = (q0_ref, q1_ref, q2_ref, q3_ref)

    def rows(k):
        return pl.ds(pl.multiple_of(plan_ref[2 * slots + k] * part, 16), part)

    def fetch(slot, k, source, index):
        src = (own_ref.at[index, rows(k)], core_ref.at[index, rows(k)], quarters[k].at[index])[source]
        return pltpu.make_async_copy(src, held.at[slot, k], in_sems.at[slot, k])

    def store(slot, k):
        return pltpu.make_async_copy(held.at[slot, k], out_ref.at[slot, rows(k)], out_sems.at[slot, k])

    for slot in range(slots):
        index = plan_ref[slots + slot]
        for source in range(3):
            @pl.when(plan_ref[slot] == source)
            def _(slot=slot, index=index, source=source):
                for k in range(NY):
                    fetch(slot, k, source, index).start()
    for slot in range(slots):
        for k in range(NY):
            fetch(slot, k, 0, 0).wait()
            store(slot, k).start()
    for slot in range(slots):
        for k in range(NY):
            store(slot, k).wait()


def branch(plan, own, other_core, quarters):
    anywhere = pl.BlockSpec(memory_space=pl.ANY)
    slots, height, width = own.shape
    return pl.pallas_call(
        branch_kernel,
        in_specs=[pl.BlockSpec(memory_space=pltpu.SMEM)] + [anywhere] * 6,
        out_specs=anywhere,
        out_shape=jax.ShapeDtypeStruct(own.shape, own.dtype),
        scratch_shapes=[
            pltpu.VMEM((slots, NY, height // NY, width), own.dtype),
            pltpu.SemaphoreType.DMA((slots, NY)),
            pltpu.SemaphoreType.DMA((slots, NY)),
        ],
        compiler_params=pltpu.CompilerParams(vmem_limit_bytes=50 * 2**20),
        cost_estimate=pl.CostEstimate(flops=0, bytes_accessed=4 * own.size, transcendentals=0),
    )(plan, own, other_core, *quarters)


def after(values, *done):
    return jax.tree.unflatten(
        jax.tree.structure(values), lax.optimization_barrier((*jax.tree.leaves(values), *done))[: len(jax.tree.leaves(values))]
    )


def cut_blocks(own, swapped, owner, x, c):
    electrons, columns = own.shape
    half, depth = electrons // NC, columns // NX

    def block(place):
        cut = [lax.dynamic_slice(a, (c * half, place * depth), (half, depth)) for a in (own, swapped)]
        return jnp.where(owner % NC == c, cut[0], cut[1])

    return [block((x + (1 - 2 * c) * dx + NX * NX) % NX) for dx in (0, 1, 3, 2)]


def scatter(blocks):
    return [lax.ppermute(sent, "walk", to_chip(dx, 0)) for dx, sent in zip((1, 3, 2), blocks[1:])]


def scattered(own, arrived, owner_x, x, c):
    for dx, block in zip((1, 3, 2), arrived):
        own = jnp.where((owner_x + (1 - 2 * c) * dx + NX * NX) % NX == x, block, own)
    return own


def flood_step(up, down):
    up, down = after((up, down))
    return lax.ppermute(up, "walk", to_chip(0, 1)), lax.ppermute(down, "walk", to_chip(0, -1))


def flooded(halves, streams, away):
    first, second = halves
    for step, (up, down) in enumerate(streams, 1):
        first = jnp.where(away == step, up, first)
        second = jnp.where(away == NZ - step, down, second)
        if step > 1:
            first = jnp.where(away == NZ - (step - 1), down, first)
            second = jnp.where(away == step - 1, up, second)
    return jnp.concatenate([first, second], axis=0)


def along_x(piece):
    return [lax.ppermute(piece, "walk", to_chip(dx, 0)) for dx in (1, 3, 2)]


def to_other_core(array):
    return lax.ppermute(array, "walk", [(i, i ^ 1) for i in range(NX * NZ * NC)])


def shards(walkers, chol, owners, branch_src):
    slots, height, _ = walkers.shape
    device, y = lax.axis_index("walk"), lax.axis_index("vec")
    x, z, c = device // (NZ * NC), device // NC % NZ, device % NC
    size = NX * NZ * NC
    total = slots * size
    own = chol[0, 0]
    owner = owners[0]
    both_ways = [
        (w * NY + v, w * NY + (v + (1 if w % NC == 0 else -1)) % NY) for w in range(size) for v in range(NY)
    ]

    def pass_on(quarter):
        return lax.ppermute(quarter, ("walk", "vec"), both_ways)

    with jax.named_scope("core_swap"):
        swapped = to_other_core(own)
    with jax.named_scope("halo_z"):
        part = height // NY
        quarter = lax.dynamic_slice_in_dim(walkers, y * part, part, 1)
        owner_x = [owner[g] // (NZ * NC) for g in range(2)]
        owner_z = [owner[g] // NC % NZ for g in range(2)]
        swapped, quarter = after((swapped, quarter))
        quarters = [lax.ppermute(quarter, "walk", across_chips())]
    with jax.named_scope("core_walkers"):
        other_core = to_other_core(after(walkers, swapped))
    with jax.named_scope("blocks"):
        blocks = [cut_blocks(own, swapped, owner[g], x, c) for g in range(2)]
    half = own.shape[0] // (2 * NC)
    is_owner = [owner_z[g] == z for g in range(2)]
    away = [((1 - 2 * c) * (z - owner_z[g]) + NZ) % NZ for g in range(2)]

    def turned(g, arrived):
        return [jnp.where(is_owner[g], halves[g][1 - i], arrived[i]) for i in range(2)]

    with jax.named_scope("x_scatter_0"):
        arrived = scatter(blocks[0])
        arrived, sent, quarters[0] = after((arrived[::-1], blocks[1], quarters[0]))
        arrived = arrived[::-1]
        piece = scattered(blocks[0][0], arrived, owner_x[0], x, c)
        halves = [(piece[:half], piece[half:])]
        halves[0], sent, quarters[0], other_core = after((halves[0], sent, quarters[0], other_core))
    with jax.named_scope("x_scatter_1"):
        arrived = scatter(sent)
    with jax.named_scope("z_flood"):
        first = flood_step(*halves[0])
    with jax.named_scope("halo_y"):
        quarters.append(pass_on(quarters[0]))
    with jax.named_scope("x_scatter_1"):
        arrived, first, quarters[1] = after((arrived, first, quarters[1]))
        piece = scattered(sent[0], arrived, owner_x[1], x, c)
        halves.append((piece[:half], piece[half:]))
    with jax.named_scope("z_flood"):
        ahead = turned(0, first)
        second = flood_step(*[jnp.stack([ahead[i], halves[1][i]]) for i in range(2)])
        late = is_owner[1] & (jnp.arange(2) == 1)[:, None, None]
        third = flood_step(*[jnp.where(late, halves[1][1 - i][None], second[i]) for i in range(2)])
    with jax.named_scope("halo_y"):
        quarters.append(pass_on(quarters[1]))
    with jax.named_scope("z_flood"):
        third, quarters[2] = after((third, quarters[2]))
        fourth = flood_step(*third)
    with jax.named_scope("halo_y"):
        quarters.append(pass_on(quarters[2]))
    with jax.named_scope("z_flood"):
        piece = flooded(halves[0], [first] + [[a[0] for a in b] for b in (second, third, fourth)], away[0])
        fifth = flood_step(*after([a[1] for a in fourth], piece))
    with jax.named_scope("x_gather_0"):
        mine = [piece] + along_x(piece)
    with jax.named_scope("z_flood"):
        piece = flooded(halves[1], [[a[1] for a in b] for b in (second, third, fourth)] + [fifth], away[1])
        piece, mine, quarters[3] = after((piece, mine[::-1], quarters[3]))
        mine = mine[::-1]
    with jax.named_scope("core_gather_0"):
        pieces = mine + [to_other_core(p) for p in mine]
        piece, pieces = after((piece, pieces))
    relative = (branch_src - (device - 1) * slots + total) % total
    side, index = relative // slots, relative % slots
    source = jnp.where(side == 1, 0, jnp.where((side == 0) == (c == 0), 2, 1))
    held = (y + jnp.arange(NY) * jnp.where(c == 0, NY - 1, 1)) % NY
    plan = after(jnp.concatenate([source, index, held]).astype(jnp.int32), pieces[-1])
    sign = 1 - 2 * c
    columns = [(x + k + NX) % NX for k in (0, -sign, sign, 2, 0, sign, -sign, 2)]
    place = jnp.stack([*columns, c, 1 - c]).astype(jnp.int32)
    with jax.named_scope("branch"):
        branched = branch(plan, walkers, other_core, quarters)
    with jax.named_scope("x_gather_1"):
        ahead = lax.ppermute(piece, "walk", to_chip(1, 0))
        later, ahead, branched = after((piece, ahead, branched))
        mine = [piece, ahead, *[lax.ppermute(later, "walk", to_chip(dx, 0)) for dx in (3, 2)]]
    with jax.named_scope("terms_0"):
        terms = [walker_terms(place, pieces, walkers)]
    with jax.named_scope("core_gather_1"):
        mine[2] = after(mine[2], terms[0])
        pieces = mine + [to_other_core(p) for p in mine]
    with jax.named_scope("terms_1"):
        terms.append(walker_terms(place, pieces, walkers))
    with jax.named_scope("results"):
        bias = jnp.stack([t[:, :2] for t in terms], axis=1).reshape(slots, -1)
        energy = sum(t[:, 2:] for t in terms)
        others = [lax.ppermute(energy, "vec", ring(NY, k)) for k in range(1, NY)]
        energy = (energy + others[1]) + (others[0] + others[2])
        row = jnp.concatenate([bias, -0.5 * energy], axis=1)
        left = lax.ppermute(row, "walk", ring(size, 1))
        right = lax.ppermute(row, "walk", ring(size, -1))
        rows = jnp.concatenate([left, row, right], axis=0)
        chosen = jnp.sum(jnp.where((relative[:, None] == jnp.arange(3 * slots))[:, :, None], rows[None], 0.0), axis=1)
        force_bias = chosen[:, :-2].reshape(slots, len(terms), 2)
    return branched, force_bias, chosen[:, -2:]


def solution(mesh):
    return jax.shard_map(
        shards,
        mesh=mesh,
        in_specs=(P("walk", None, None), P("vec", "walk", None, None), P("vec", None), P("walk")),
        out_specs=(P("walk", None, None), P("walk", "vec", None), P("walk", None)),
        check_vma=False,
    )
```
